32 devices in a mesh: pair: 8 (over y, x, core), ladder: 4 (over z).
Axes of the slice: x: 2, y: 2, z: 4, core: 2. Of those that a mesh axis runs over, the one named last changes fastest.
Arguments:
- factors: bfloat16 [1536, 512, 512], P('pair', 'ladder'), may hold values from -0.0625 to 0.0625
- lambdas: bfloat16 [4, 512, 512], P(None, 'pair'), may hold values from -6 to 6
Outputs:
- residual: bfloat16 [512, 4, 512], P('pair', None, 'ladder')
The draws below stay inside these ranges and needn't reach their ends.
All inputs are finite; a program needn't handle non-finite values.
Results may differ from the reference program's by a relative error of at most 0.013.
Values may be sent and summed in bfloat16 or wider, within the bound.
No kernel may reach another device: no remote copies, remote signals or barrier semaphores. Data moves between devices by JAX's collectives and lax.ppermute only.
A program may use at most 256 MiB of HBM per device.

```python
import jax
import jax.numpy as jnp
from jax import lax

V = 512
NAUX = 1536
NPAIR = 4


def with_spikes(result, stream_key, source, target, shards_of, factor):
    def block_of(axis_at):
        return (jnp.arange(result.shape[axis_at]) // (result.shape[axis_at] // shards_of)).reshape((-1,) + (1,) * (result.ndim - 1 - axis_at))

    first = jax.random.permutation(stream_key, shards_of)[block_of(target)]
    second = (block_of(target) + shards_of // 2) % shards_of
    return jnp.where((block_of(source) == first) | (block_of(source) == second), factor * result, result)


def block_scale(rng, extent, pieces, low, high):
    level = 1.0
    for dim, blocks in pieces:
        heights = jax.random.uniform(jax.random.fold_in(jax.random.fold_in(rng, 6), dim), (blocks,), jnp.float32, low / len(pieces), high / len(pieces))
        level = level * jnp.repeat(jnp.exp(heights), extent[dim] // blocks).reshape((-1,) + (1,) * (len(extent) - 1 - dim))
    return level


def bell_draw(rng, shape, deviation, bound, shards=(), held_as=jnp.bfloat16):
    result = deviation * jax.random.normal(rng, shape, jnp.float32)
    if shards:
        result = result * block_scale(rng, shape, shards, -0.22, 0.18)
    return jnp.clip(result, -bound, bound).astype(held_as)


def heavy_noise(own_key, dims, spread, most, split, heavy, kind=jnp.bfloat16):
    values = spread * jax.random.normal(own_key, dims, jnp.float32)
    if split:
        values = values * block_scale(own_key, dims, split, -0.22, 0.18)
    return jnp.clip(with_spikes(values, jax.random.fold_in(own_key, 3), *heavy), -most, most).astype(kind)


def setup_inputs(seed: int = 0) -> dict:
    arg_keys = jax.random.split(jax.random.key(seed), 3)
    return {
        "factors": heavy_noise(arg_keys[0], (NAUX, V, V), (V * 40) ** -0.5, 0.0625, ((0, 8), (1, 4)), (0, 1, 8, 2.0)),
        "lambdas": bell_draw(arg_keys[1], (NPAIR, V, V), 1.0, 6.0, ((1, 8),)),
    }


def reference(factors, lambdas):
    lam_wide = lambdas.astype(jnp.float32)
    step_size = min(NAUX, 64)

    def accumulate(running, index):
        ladder_part, cycle_part = running
        aux_block = lax.dynamic_slice_in_dim(factors, (index * step_size).astype(jnp.int32), step_size, 0).astype(jnp.float32)
        half_done = jnp.einsum('pac,ncd->npad', aux_block, lam_wide, precision=lax.Precision.HIGHEST).astype(jnp.bfloat16)
        half_done = lax.optimization_barrier(half_done).astype(jnp.float32)
        ladder_part = ladder_part + jnp.einsum('npad,pbd->bna', half_done, aux_block, precision=lax.Precision.HIGHEST)
        weights = jnp.einsum('pcd,ncd->p', aux_block, lam_wide, precision=lax.Precision.HIGHEST)
        cycle_part = cycle_part + jnp.einsum('p,pab->ab', weights, aux_block, precision=lax.Precision.HIGHEST)
        return (ladder_part, cycle_part), None

    start_state = (jnp.zeros((V, NPAIR, V), jnp.float32), jnp.zeros((V, V), jnp.float32))
    (ladder_part, cycle_part), _ = lax.scan(accumulate, start_state, jnp.arange(NAUX // step_size, dtype=jnp.int32))
    cycle_rounded = lax.optimization_barrier(cycle_part.astype(jnp.bfloat16)).astype(jnp.float32)
    cycle_term = jnp.einsum('ae,neb->bna', cycle_rounded, lam_wide, precision=lax.Precision.HIGHEST)
    cycle_scale = float(NPAIR * V) ** -0.5
    return (ladder_part + cycle_scale * cycle_term).astype(jnp.bfloat16)
```

```python
import functools

import jax
import jax.numpy as jnp
from jax import lax
from jax.sharding import PartitionSpec as P

F32 = jnp.float32
BF16 = jnp.bfloat16


def chunk_sizes(per_hub):
    sizes = []
    left = per_hub
    for share in (6, 24, 12, 4):
        size = min(left, max(1, share * per_hub // 48))
        if size:
            sizes.append(size)
            left -= size
    if left:
        sizes.append(left)
    return sizes


def radices(count):
    steps = []
    while count > 1:
        step = 2 if not steps and count % 2 == 0 else next(r for r in (4, 2, 3, 5, count) if count % r == 0)
        steps.append(step)
        count //= step
    return steps


def exchange_sum(blocks, axis, index, size, stride, radix):
    digit = index // stride % radix
    total = lax.dynamic_index_in_dim(blocks, digit, 0, keepdims=False)
    for shift in range(1, radix):
        perm = []
        for source in range(size):
            own = source // stride % radix
            perm.append((source, source + ((own + shift) % radix - own) * stride))
        outgoing = lax.dynamic_index_in_dim(blocks, (digit + shift) % radix, 0, keepdims=False)
        total = total + lax.ppermute(outgoing.astype(BF16), axis, perm).astype(F32)
    return total


def per_device(pair_size, ladder_size, factors, lambdas):
    own_aux, rows, virt = factors.shape
    pairs = lambdas.shape[0]
    per_hub = own_aux // ladder_size
    pair_index = lax.axis_index("pair")
    ladder_index = lax.axis_index("ladder")
    cycle_scale = float(pairs * virt) ** (-0.5)
    cols = virt // pair_size

    lam_all = lax.all_gather(lambdas, "pair", axis=1, tiled=True)

    lam_sum = jnp.sum(
        lax.dynamic_slice_in_dim(lam_all, ladder_index * rows, rows, 1).astype(F32), axis=0
    )
    weights = lax.psum(jnp.sum(factors.astype(F32) * lam_sum[None], axis=(1, 2)), "ladder")
    cycle = lax.psum(jnp.sum(weights[:, None, None] * factors.astype(F32), axis=0), "pair")
    lam_cols = lax.dynamic_slice_in_dim(lam_all, pair_index * cols, cols, 2)
    cycle_term = cycle_scale * jnp.einsum(
        "ae,neb->bna", cycle.astype(BF16), lam_cols, preferred_element_type=F32
    )
    lam_all, cycle_term = lax.optimization_barrier((lam_all, cycle_term))

    arrived = []
    start = 0
    total = None
    for place, size in enumerate(chunk_sizes(per_hub)):
        part = lax.slice_in_dim(factors, start, start + size * ladder_size, axis=0)
        part = part.reshape(ladder_size, size, rows, virt)
        if place >= 2:
            part, arrived[place - 2] = lax.optimization_barrier((part, arrived[place - 2]))
        arrived.append(lax.all_to_all(part, "ladder", split_axis=0, concat_axis=0, tiled=True))
        start += size * ladder_size
    for block in arrived:
        half = jnp.einsum("jpac,ncd->njpad", block, lam_all, preferred_element_type=F32).astype(BF16)
        piece = jnp.einsum("njpad,kpbd->kbnja", half, block, preferred_element_type=F32)
        total = piece if total is None else total + piece
        total, lam_all = lax.optimization_barrier((total, lam_all))
    total = total.reshape(virt, pairs, virt)

    stride = 1
    outer = pair_size
    for radix in radices(pair_size):
        outer //= radix
        blocks = jnp.moveaxis(total.reshape(outer, radix, cols, pairs, virt), 1, 0)
        total = exchange_sum(blocks, "pair", pair_index, pair_size, stride, radix)
        stride *= radix
    total = total.reshape(cols, pairs, ladder_size, rows)
    total = exchange_sum(jnp.moveaxis(total, 2, 0), "ladder", ladder_index, ladder_size, 1, ladder_size)
    return (total + cycle_term).astype(BF16)


def solution(mesh):
    in_specs = (P("pair", "ladder", None), P(None, "pair", None))
    out_specs = P("pair", None, "ladder")
    body = functools.partial(per_device, mesh.shape["pair"], mesh.shape["ladder"])
    return jax.shard_map(body, mesh=mesh, in_specs=in_specs, out_specs=out_specs, check_vma=False)
```

```python
import functools

import jax
import jax.numpy as jnp
from jax import lax
from jax.sharding import PartitionSpec as P

F32 = jnp.float32
BF16 = jnp.bfloat16


def chunk_sizes(per_hub):
    sizes = []
    left = per_hub
    for share in (4, 20, 14, 6, 3):
        size = min(left, max(1, share * per_hub // 48))
        if size:
            sizes.append(size)
            left -= size
    if left:
        sizes.append(left)
    return sizes


def radices(count):
    steps = []
    while count > 1:
        step = 2 if not steps and count % 2 == 0 else next(r for r in (4, 2, 3, 5, count) if count % r == 0)
        steps.append(step)
        count //= step
    return steps


def turned(size, stride, radix, shift):
    perm = []
    for source in range(size):
        digit = source // stride % radix
        perm.append((source, source + ((digit + shift) % radix - digit) * stride))
    return perm


def per_device(pair_size, ladder_size, factors, lambdas):
    own_aux, rows, virt = factors.shape
    pairs = lambdas.shape[0]
    pair_index = lax.axis_index("pair")
    ladder_index = lax.axis_index("ladder")
    cycle_scale = float(pairs * virt) ** (-0.5)
    cols = virt // pair_size
    sizes = chunk_sizes(own_aux // ladder_size)
    starts = [ladder_size * sum(sizes[:place]) for place in range(len(sizes))]

    def ladder_shift(array, shift):
        return lax.ppermute(array, "ladder", turned(ladder_size, 1, ladder_size, shift))

    def exchange(place, index):
        size = sizes[place]
        blocks = []
        for shift in range(ladder_size):
            hub = (index + shift) % ladder_size
            block = lax.dynamic_slice_in_dim(factors, starts[place] + hub * size, size, 0)
            blocks.append(ladder_shift(block, shift) if shift else block)
        return blocks

    blocks = [exchange(0, ladder_index)]
    lam_all = lax.all_gather(lambdas, "pair", axis=1, tiled=True)
    index, lam_all = lax.optimization_barrier((ladder_index, lam_all))
    blocks.append(exchange(1, index))

    lam_sum = jnp.sum(
        lax.dynamic_slice_in_dim(lam_all, ladder_index * rows, rows, 1).astype(F32), axis=0
    )
    weights = jnp.sum(factors.astype(F32) * lam_sum[None], axis=(1, 2))
    weight_parts = [weights] + [ladder_shift(weights, shift) for shift in range(1, ladder_size)]

    total = None
    cycle_term = None
    for place in range(len(sizes)):
        if place + 2 < len(sizes):
            index, *blocks[place] = lax.optimization_barrier((index, *blocks[place]))
            blocks.append(exchange(place + 2, index))
        block = jnp.concatenate(blocks[place], axis=1)
        half = jnp.einsum("pac,ncd->npad", block, lam_all, preferred_element_type=F32).astype(BF16)
        piece = jnp.einsum("npad,pbd->nba", half, block, preferred_element_type=F32)
        total = piece if total is None else total + piece
        if place == 0:
            total, *weight_parts = lax.optimization_barrier((total, *weight_parts))
            cycle = lax.psum(
                jnp.sum(sum(weight_parts)[:, None, None] * factors.astype(F32), axis=0), "pair"
            )
            lam_cols = lax.dynamic_slice_in_dim(lam_all, pair_index * cols, cols, 2)
            cycle_term = cycle_scale * jnp.einsum(
                "ae,neb->nba", cycle.astype(BF16), lam_cols, preferred_element_type=F32
            )
            total, lam_all, cycle_term = lax.optimization_barrier((total, lam_all, cycle_term))
        else:
            total, lam_all = lax.optimization_barrier((total, lam_all))

    stride = 1
    low = pair_size // ladder_size
    for radix in radices(low):
        low //= radix
        digit = pair_index // stride % radix
        view = total.reshape(pairs, ladder_size, low, radix, cols, virt)
        total = lax.dynamic_index_in_dim(view, digit, 3, keepdims=False)
        for shift in range(1, radix):
            part = lax.dynamic_index_in_dim(view, (digit + shift) % radix, 3, keepdims=False)
            part = lax.ppermute(part.astype(BF16), "pair", turned(pair_size, stride, radix, shift))
            total = total + part.astype(F32)
        stride *= radix
    digit = pair_index // stride
    view = total.reshape(pairs, ladder_size, cols, virt)
    total = None
    for shift in range(ladder_size):
        turn = (ladder_index - digit - shift) % ladder_size
        part = lax.dynamic_index_in_dim(view, turn, 1, keepdims=False)
        if shift:
            perm = turned(pair_size, stride, ladder_size, shift)
            part = lax.ppermute(part.astype(BF16), "pair", perm).astype(F32)
        total = part if total is None else total + part

    result = cycle_term
    for turn in range(ladder_size):
        part = lax.slice_in_dim(total, turn * rows, (turn + 1) * rows, axis=2)
        if turn:
            part = ladder_shift(part.astype(BF16), ladder_size - turn).astype(F32)
        result = result + part
    return jnp.swapaxes(result.astype(BF16), 0, 1)


def solution(mesh):
    in_specs = (P("pair", "ladder", None), P(None, "pair", None))
    out_specs = P("pair", None, "ladder")
    body = functools.partial(per_device, mesh.shape["pair"], mesh.shape["ladder"])
    return jax.shard_map(body, mesh=mesh, in_specs=in_specs, out_specs=out_specs, check_vma=False)
```

```python
import functools

import jax
import jax.numpy as jnp
from jax import lax
from jax.sharding import PartitionSpec as P

F32 = jnp.float32
BF16 = jnp.bfloat16
WINDOW = 4


def chunk_sizes(per_hub):
    sizes = []
    left = per_hub
    for share in (5, 20, 13, 6, 3):
        size = min(left, max(1, share * per_hub // 48))
        if size:
            sizes.append(size)
            left -= size
    if left:
        sizes.append(left)
    return sizes


def radices(count):
    steps = []
    while count > 1:
        step = 2 if not steps and count % 2 == 0 else next(r for r in (4, 2, 3, 5, count) if count % r == 0)
        steps.append(step)
        count //= step
    return steps


def turned(size, stride, radix, shift):
    perm = []
    for source in range(size):
        digit = source // stride % radix
        perm.append((source, source + ((digit + shift) % radix - digit) * stride))
    return perm


def per_device(pair_size, ladder_size, factors, lambdas):
    own_aux, rows, virt = factors.shape
    pairs = lambdas.shape[0]
    pair_index = lax.axis_index("pair")
    ladder_index = lax.axis_index("ladder")
    cycle_scale = float(pairs * virt) ** (-0.5)
    cols = virt // pair_size
    sizes = chunk_sizes(own_aux // ladder_size)
    starts = [ladder_size * sum(sizes[:place]) for place in range(len(sizes))]

    def ladder_shift(array, shift):
        return lax.ppermute(array, "ladder", turned(ladder_size, 1, ladder_size, shift))

    def cut(place, index):
        size = sizes[place]
        hubs = [(index + shift) % ladder_size for shift in range(ladder_size)]
        return [lax.dynamic_slice_in_dim(factors, starts[place] + hub * size, size, 0) for hub in hubs]

    blocks = []
    stream = []

    def exchange(parts):
        blocks.append(parts[:1])
        for shift in range(1, ladder_size):
            part = parts[shift]
            if len(stream) >= WINDOW:
                place, at = stream[len(stream) - WINDOW]
                part, blocks[place][at] = lax.optimization_barrier((part, blocks[place][at]))
            stream.append((len(blocks) - 1, shift))
            blocks[-1].append(ladder_shift(part, shift))

    first = cut(0, ladder_index)
    index, first = lax.optimization_barrier((ladder_index, first))
    exchange(first)
    exchange(cut(1, index))
    lam_all = lax.all_gather(lambdas, "pair", axis=1, tiled=True)

    lam_sum = jnp.sum(
        lax.dynamic_slice_in_dim(lam_all, ladder_index * rows, rows, 1).astype(F32), axis=0
    )
    weights = jnp.sum(factors.astype(F32) * lam_sum[None], axis=(1, 2))
    index, weights = lax.optimization_barrier((index, weights))
    weights = lax.all_to_all(
        jnp.broadcast_to(weights, (ladder_size, own_aux)), "ladder", split_axis=0, concat_axis=0
    )
    for place in range(2, len(sizes)):
        exchange(cut(place, index))

    total = None
    cycle_term = None
    for place in range(len(sizes)):
        block = jnp.concatenate(blocks[place], axis=1)
        half = jnp.einsum("pac,ncd->npad", block, lam_all, preferred_element_type=F32).astype(BF16)
        piece = jnp.einsum("npad,pbd->nba", half, block, preferred_element_type=F32)
        total = piece if total is None else total + piece
        if place == 1:
            total, weights = lax.optimization_barrier((total, weights))
            weights = jnp.sum(weights, axis=0)
            cycle = lax.psum(jnp.sum(weights[:, None, None] * factors.astype(F32), axis=0), "pair")
            lam_cols = lax.dynamic_slice_in_dim(lam_all, pair_index * cols, cols, 2)
            cycle_term = cycle_scale * jnp.einsum(
                "ae,neb->nba", cycle.astype(BF16), lam_cols, preferred_element_type=F32
            )
            total, lam_all, cycle_term = lax.optimization_barrier((total, lam_all, cycle_term))
        else:
            total, lam_all = lax.optimization_barrier((total, lam_all))

    stride = 1
    low = pair_size // ladder_size
    for radix in radices(low):
        low //= radix
        digit = pair_index // stride % radix
        view = total.reshape(pairs, ladder_size, low, radix, cols, virt)
        total = lax.dynamic_index_in_dim(view, digit, 3, keepdims=False)
        for shift in range(1, radix):
            part = lax.dynamic_index_in_dim(view, (digit + shift) % radix, 3, keepdims=False)
            part = lax.ppermute(part.astype(BF16), "pair", turned(pair_size, stride, radix, shift))
            total = total + part.astype(F32)
        stride *= radix
    digit = pair_index // stride
    view = total.reshape(pairs, ladder_size, cols, virt)
    total = None
    for shift in range(ladder_size):
        turn = (ladder_index - digit - shift) % ladder_size
        part = lax.dynamic_index_in_dim(view, turn, 1, keepdims=False)
        if shift:
            perm = turned(pair_size, stride, ladder_size, shift)
            part = lax.ppermute(part.astype(BF16), "pair", perm).astype(F32)
        total = part if total is None else total + part

    result = cycle_term
    for turn in range(ladder_size):
        part = lax.slice_in_dim(total, turn * rows, (turn + 1) * rows, axis=2)
        if turn:
            part = ladder_shift(part.astype(BF16), ladder_size - turn).astype(F32)
        result = result + part
    return jnp.swapaxes(result.astype(BF16), 0, 1)


def solution(mesh):
    in_specs = (P("pair", "ladder", None), P(None, "pair", None))
    out_specs = P("pair", None, "ladder")
    body = functools.partial(per_device, mesh.shape["pair"], mesh.shape["ladder"])
    return jax.shard_map(body, mesh=mesh, in_specs=in_specs, out_specs=out_specs, check_vma=False)
```

```python
import functools

import jax
import jax.numpy as jnp
from jax import lax
from jax.sharding import PartitionSpec as P

F32 = jnp.float32
BF16 = jnp.bfloat16


def chunk_sizes(per_hub):
    sizes = []
    left = per_hub
    for share in (2, 5, 20, 12, 5, 3):
        size = min(left, max(1, share * per_hub // 48))
        if size:
            sizes.append(size)
            left -= size
    if left:
        sizes.append(left)
    return sizes


def radices(count):
    steps = []
    while count > 1:
        step = 2 if not steps and count % 2 == 0 else next(r for r in (4, 2, 3, 5, count) if count % r == 0)
        steps.append(step)
        count //= step
    return steps


def turned(size, stride, radix, shift):
    perm = []
    for source in range(size):
        digit = source // stride % radix
        perm.append((source, source + ((digit + shift) % radix - digit) * stride))
    return perm


def per_device(pair_size, ladder_size, factors, lambdas):
    own_aux, rows, virt = factors.shape
    pairs = lambdas.shape[0]
    pair_index = lax.axis_index("pair")
    ladder_index = lax.axis_index("ladder")
    cycle_scale = float(pairs * virt) ** (-0.5)
    cols = virt // pair_size
    sizes = chunk_sizes(own_aux // ladder_size)
    starts = [ladder_size * sum(sizes[:place]) for place in range(len(sizes))]

    def ladder_shift(array, shift):
        return lax.ppermute(array, "ladder", turned(ladder_size, 1, ladder_size, shift))

    def cut(place, index):
        size = sizes[place]
        hubs = [(index + shift) % ladder_size for shift in range(ladder_size)]
        return [lax.dynamic_slice_in_dim(factors, starts[place] + hub * size, size, 0) for hub in hubs]

    def exchange(parts):
        return [ladder_shift(part, shift) if shift else part for shift, part in enumerate(parts)]

    first = cut(0, ladder_index)
    blocks = [exchange(first)]
    index, first = lax.optimization_barrier((ladder_index, first))
    blocks.append(exchange(cut(1, index)))
    lam_all = lax.all_gather(lambdas, "pair", axis=1, tiled=True)
    index, lam_all = lax.optimization_barrier((index, lam_all))
    third = cut(2, index)
    lam_all, third = lax.optimization_barrier((lam_all, third))

    lam_sum = jnp.sum(
        lax.dynamic_slice_in_dim(lam_all, ladder_index * rows, rows, 1).astype(F32), axis=0
    )
    weights = jnp.sum(factors.astype(F32) * lam_sum[None], axis=(1, 2))
    weights = lax.all_to_all(
        jnp.broadcast_to(weights, (ladder_size, own_aux)), "ladder", split_axis=0, concat_axis=0
    )

    total = None
    cycle_term = None
    for place in range(len(sizes)):
        if place + 2 < len(sizes):
            if place == 0:
                third, blocks[0] = lax.optimization_barrier((third, blocks[0]))
            else:
                index, blocks[place] = lax.optimization_barrier((index, blocks[place]))
                third = cut(place + 2, index)
            blocks.append(exchange(third))
        block = jnp.concatenate(blocks[place], axis=1)
        half = jnp.einsum("pac,ncd->npad", block, lam_all, preferred_element_type=F32).astype(BF16)
        piece = jnp.einsum("npad,pbd->nba", half, block, preferred_element_type=F32)
        total = piece if total is None else total + piece
        if place == 2:
            total, weights = lax.optimization_barrier((total, weights))
            weights = jnp.sum(weights, axis=0)
            cycle = lax.psum(jnp.sum(weights[:, None, None] * factors.astype(F32), axis=0), "pair")
            lam_cols = lax.dynamic_slice_in_dim(lam_all, pair_index * cols, cols, 2)
            cycle_term = cycle_scale * jnp.einsum(
                "ae,neb->nba", cycle.astype(BF16), lam_cols, preferred_element_type=F32
            )
            total, lam_all, cycle_term = lax.optimization_barrier((total, lam_all, cycle_term))
        else:
            total, lam_all = lax.optimization_barrier((total, lam_all))

    stride = 1
    low = pair_size // ladder_size
    for radix in radices(low):
        low //= radix
        digit = pair_index // stride % radix
        view = total.reshape(pairs, ladder_size, low, radix, cols, virt)
        total = lax.dynamic_index_in_dim(view, digit, 3, keepdims=False)
        for shift in range(1, radix):
            part = lax.dynamic_index_in_dim(view, (digit + shift) % radix, 3, keepdims=False)
            part = lax.ppermute(part.astype(BF16), "pair", turned(pair_size, stride, radix, shift))
            total = total + part.astype(F32)
        stride *= radix
    digit = pair_index // stride
    view = total.reshape(pairs, ladder_size, cols, virt)
    total = None
    for shift in range(ladder_size):
        turn = (ladder_index - digit - shift) % ladder_size
        part = lax.dynamic_index_in_dim(view, turn, 1, keepdims=False)
        if shift:
            perm = turned(pair_size, stride, ladder_size, shift)
            part = lax.ppermute(part.astype(BF16), "pair", perm).astype(F32)
        total = part if total is None else total + part

    result = cycle_term
    for turn in range(ladder_size):
        part = lax.slice_in_dim(total, turn * rows, (turn + 1) * rows, axis=2)
        if turn:
            part = ladder_shift(part.astype(BF16), ladder_size - turn).astype(F32)
        result = result + part
    return jnp.swapaxes(result.astype(BF16), 0, 1)


def solution(mesh):
    in_specs = (P("pair", "ladder", None), P(None, "pair", None))
    out_specs = P("pair", None, "ladder")
    body = functools.partial(per_device, mesh.shape["pair"], mesh.shape["ladder"])
    return jax.shard_map(body, mesh=mesh, in_specs=in_specs, out_specs=out_specs, check_vma=False)
```

```python
import functools

import jax
import jax.numpy as jnp
from jax import lax
from jax.sharding import PartitionSpec as P

F32 = jnp.float32
BF16 = jnp.bfloat16


def chunk_sizes(per_hub):
    sizes = []
    left = per_hub
    for share in (5, 20, 13, 6, 3):
        size = min(left, max(1, share * per_hub // 48))
        if size:
            sizes.append(size)
            left -= size
    if left:
        sizes.append(left)
    return sizes


def radices(count):
    steps = []
    while count > 1:
        step = 2 if not steps and count % 2 == 0 else next(r for r in (4, 2, 3, 5, count) if count % r == 0)
        steps.append(step)
        count //= step
    return steps


def turned(size, stride, radix, shift):
    perm = []
    for source in range(size):
        digit = source // stride % radix
        perm.append((source, source + ((digit + shift) % radix - digit) * stride))
    return perm


def per_device(pair_size, ladder_size, factors, lambdas):
    own_aux, rows, virt = factors.shape
    pairs = lambdas.shape[0]
    pair_index = lax.axis_index("pair")
    ladder_index = lax.axis_index("ladder")
    cycle_scale = float(pairs * virt) ** (-0.5)
    cols = virt // pair_size
    sizes = chunk_sizes(own_aux // ladder_size)
    starts = [ladder_size * sum(sizes[:place]) for place in range(len(sizes))]

    def ladder_shift(array, shift):
        return lax.ppermute(array, "ladder", turned(ladder_size, 1, ladder_size, shift))

    def cut(place, index):
        size = sizes[place]
        hubs = [(index + shift) % ladder_size for shift in range(ladder_size)]
        return [lax.dynamic_slice_in_dim(factors, starts[place] + hub * size, size, 0) for hub in hubs]

    def exchange(parts):
        return [ladder_shift(part, shift) if shift else part for shift, part in enumerate(parts)]

    first = cut(0, ladder_index)
    blocks = [exchange(first)]
    lam_all = lax.all_gather(lambdas, "pair", axis=1, tiled=True)
    index, first = lax.optimization_barrier((ladder_index, first))
    second = cut(1, index)
    lam_all, second = lax.optimization_barrier((lam_all, second))

    lam_sum = jnp.sum(
        lax.dynamic_slice_in_dim(lam_all, ladder_index * rows, rows, 1).astype(F32), axis=0
    )
    weights = lax.psum(jnp.sum(factors.astype(F32) * lam_sum[None], axis=(1, 2)), "ladder")
    index, weights, second = lax.optimization_barrier((index, weights, second))
    blocks.append(exchange(second))

    total = None
    cycle_term = None
    for place in range(len(sizes)):
        if place + 2 < len(sizes):
            index, blocks[place] = lax.optimization_barrier((index, blocks[place]))
            blocks.append(exchange(cut(place + 2, index)))
        block = jnp.concatenate(blocks[place], axis=1)
        half = jnp.einsum("pac,ncd->npad", block, lam_all, preferred_element_type=F32).astype(BF16)
        piece = jnp.einsum("npad,pbd->nba", half, block, preferred_element_type=F32)
        total = piece if total is None else total + piece
        if place == 0:
            total, weights = lax.optimization_barrier((total, weights))
            cycle = lax.psum(jnp.sum(weights[:, None, None] * factors.astype(F32), axis=0), "pair")
            lam_cols = lax.dynamic_slice_in_dim(lam_all, pair_index * cols, cols, 2)
            cycle_term = cycle_scale * jnp.einsum(
                "ae,neb->nba", cycle.astype(BF16), lam_cols, preferred_element_type=F32
            )
            total, lam_all, cycle_term = lax.optimization_barrier((total, lam_all, cycle_term))
        else:
            total, lam_all = lax.optimization_barrier((total, lam_all))

    stride = 1
    low = pair_size // ladder_size
    for radix in radices(low):
        low //= radix
        digit = pair_index // stride % radix
        view = total.reshape(pairs, ladder_size, low, radix, cols, virt)
        total = lax.dynamic_index_in_dim(view, digit, 3, keepdims=False)
        for shift in range(1, radix):
            part = lax.dynamic_index_in_dim(view, (digit + shift) % radix, 3, keepdims=False)
            part = lax.ppermute(part.astype(BF16), "pair", turned(pair_size, stride, radix, shift))
            total = total + part.astype(F32)
        stride *= radix
    digit = pair_index // stride
    view = total.reshape(pairs, ladder_size, cols, virt)
    total = None
    for shift in range(ladder_size):
        turn = (ladder_index - digit - shift) % ladder_size
        part = lax.dynamic_index_in_dim(view, turn, 1, keepdims=False)
        if shift:
            perm = turned(pair_size, stride, ladder_size, shift)
            part = lax.ppermute(part.astype(BF16), "pair", perm).astype(F32)
        total = part if total is None else total + part

    result = cycle_term
    for turn in range(ladder_size):
        part = lax.slice_in_dim(total, turn * rows, (turn + 1) * rows, axis=2)
        if turn:
            part = ladder_shift(part.astype(BF16), ladder_size - turn).astype(F32)
        result = result + part
    return jnp.swapaxes(result.astype(BF16), 0, 1)


def solution(mesh):
    in_specs = (P("pair", "ladder", None), P(None, "pair", None))
    out_specs = P("pair", None, "ladder")
    body = functools.partial(per_device, mesh.shape["pair"], mesh.shape["ladder"])
    return jax.shard_map(body, mesh=mesh, in_specs=in_specs, out_specs=out_specs, check_vma=False)
```

```python
import functools

import jax
import jax.numpy as jnp
from jax import lax
from jax.experimental import pallas as pl
from jax.experimental.pallas import tpu as pltpu
from jax.sharding import PartitionSpec as P

F32 = jnp.float32
BF16 = jnp.bfloat16


def chunk_sizes(per_hub):
    sizes = []
    left = per_hub
    for share in (5, 20, 13, 6, 3):
        size = min(left, max(1, share * per_hub // 48))
        if size:
            sizes.append(size)
            left -= size
    if left:
        sizes.append(left)
    return sizes


def radices(count):
    steps = []
    while count > 1:
        step = 2 if not steps and count % 2 == 0 else next(r for r in (4, 2, 3, 5, count) if count % r == 0)
        steps.append(step)
        count //= step
    return steps


def turned(size, stride, radix, shift):
    perm = []
    for source in range(size):
        digit = source // stride % radix
        perm.append((source, source + ((digit + shift) % radix - digit) * stride))
    return perm


def products_kernel(count, *refs):
    parts = refs[:count]
    lam_ref, start_ref = refs[count : count + 2] if len(refs) == count + 4 else (refs[count], None)
    total_ref, block_ref = refs[-2:]
    rows = parts[0].shape[1]
    pairs = lam_ref.shape[0]

    @pl.when(pl.program_id(0) == 0)
    def _():
        total_ref[...] = jnp.zeros_like(total_ref) if start_ref is None else start_ref[...]

    for at, part in enumerate(parts):
        block_ref[at * rows : (at + 1) * rows, :] = part[0]

    def one_pair(pair, carry):
        block = block_ref[...]
        half = lax.dot_general(
            lam_ref[pair], block, (((1,), (1,)), ((), ())), preferred_element_type=F32
        ).astype(BF16)
        total_ref[pair] += jnp.dot(block, half, preferred_element_type=F32)
        return carry

    lax.fori_loop(0, pairs, one_pair, 0)


def products(parts, lam_turned, total):
    size, rows, virt = parts[0].shape
    pairs = lam_turned.shape[0]
    count = len(parts)
    whole = pl.BlockSpec((pairs, virt, virt), lambda p: (0, 0, 0))
    operands = [*parts, lam_turned] + ([] if total is None else [total])
    return pl.pallas_call(
        functools.partial(products_kernel, count),
        grid=(size,),
        in_specs=[pl.BlockSpec((1, rows, virt), lambda p: (p, 0, 0))] * count
        + [whole] * (len(operands) - count),
        out_specs=whole,
        out_shape=jax.ShapeDtypeStruct((pairs, virt, virt), F32),
        scratch_shapes=[pltpu.VMEM((virt, virt), BF16)],
        input_output_aliases={} if total is None else {count + 1: 0},
        compiler_params=pltpu.CompilerParams(vmem_limit_bytes=40 << 20),
        cost_estimate=pl.CostEstimate(flops=size << 20, bytes_accessed=1 << 20, transcendentals=0),
    )(*operands)


def per_device(pair_size, ladder_size, factors, lambdas):
    own_aux, rows, virt = factors.shape
    pairs = lambdas.shape[0]
    pair_index = lax.axis_index("pair")
    ladder_index = lax.axis_index("ladder")
    cycle_scale = float(pairs * virt) ** (-0.5)
    cols = virt // pair_size
    sizes = chunk_sizes(own_aux // ladder_size)
    starts = [ladder_size * sum(sizes[:place]) for place in range(len(sizes))]

    def ladder_shift(array, shift):
        return lax.ppermute(array, "ladder", turned(ladder_size, 1, ladder_size, shift))

    def cut(place, index):
        size = sizes[place]
        hubs = [(index + shift) % ladder_size for shift in range(ladder_size)]
        return [lax.dynamic_slice_in_dim(factors, starts[place] + hub * size, size, 0) for hub in hubs]

    def exchange(parts):
        return [ladder_shift(part, shift) if shift else part for shift, part in enumerate(parts)]

    first = cut(0, ladder_index)
    blocks = [exchange(first)]
    lam_all = lax.all_gather(lambdas, "pair", axis=1, tiled=True)
    index, first = lax.optimization_barrier((ladder_index, first))
    second = cut(1, index)
    lam_all, second = lax.optimization_barrier((lam_all, second))

    lam_sum = jnp.sum(
        lax.dynamic_slice_in_dim(lam_all, ladder_index * rows, rows, 1).astype(F32), axis=0
    )
    weights = lax.psum(jnp.sum(factors.astype(F32) * lam_sum[None], axis=(1, 2)), "ladder")
    index, weights, second = lax.optimization_barrier((index, weights, second))
    blocks.append(exchange(second))

    lam_turned = jnp.swapaxes(lam_all, 1, 2)
    total = None
    cycle_term = None
    for place in range(len(sizes)):
        if place + 2 < len(sizes):
            if place:
                index, total = lax.optimization_barrier((index, total))
            index, blocks[place] = lax.optimization_barrier((index, blocks[place]))
            blocks.append(exchange(cut(place + 2, index)))
        total = products(blocks[place], lam_turned, total)
        if place == 0:
            total, weights = lax.optimization_barrier((total, weights))
            cycle = lax.psum(jnp.sum(weights[:, None, None] * factors.astype(F32), axis=0), "pair")
            lam_cols = lax.dynamic_slice_in_dim(lam_all, pair_index * cols, cols, 2)
            cycle_term = cycle_scale * jnp.einsum(
                "ae,neb->nba", cycle.astype(BF16), lam_cols, preferred_element_type=F32
            )
            total, cycle_term = lax.optimization_barrier((total, cycle_term))

    stride = 1
    low = pair_size // ladder_size
    for radix in radices(low):
        low //= radix
        digit = pair_index // stride % radix
        view = total.reshape(pairs, ladder_size, low, radix, cols, virt)
        total = lax.dynamic_index_in_dim(view, digit, 3, keepdims=False)
        for shift in range(1, radix):
            part = lax.dynamic_index_in_dim(view, (digit + shift) % radix, 3, keepdims=False)
            part = lax.ppermute(part.astype(BF16), "pair", turned(pair_size, stride, radix, shift))
            total = total + part.astype(F32)
        stride *= radix
    digit = pair_index // stride
    view = total.reshape(pairs, ladder_size, cols, virt)
    total = None
    for shift in range(ladder_size):
        turn = (ladder_index - digit - shift) % ladder_size
        part = lax.dynamic_index_in_dim(view, turn, 1, keepdims=False)
        if shift:
            perm = turned(pair_size, stride, ladder_size, shift)
            part = lax.ppermute(part.astype(BF16), "pair", perm).astype(F32)
        total = part if total is None else total + part

    result = cycle_term
    for turn in range(ladder_size):
        part = lax.slice_in_dim(total, turn * rows, (turn + 1) * rows, axis=2)
        if turn:
            part = ladder_shift(part.astype(BF16), ladder_size - turn).astype(F32)
        result = result + part
    return jnp.swapaxes(result.astype(BF16), 0, 1)


def solution(mesh):
    in_specs = (P("pair", "ladder", None), P(None, "pair", None))
    out_specs = P("pair", None, "ladder")
    body = functools.partial(per_device, mesh.shape["pair"], mesh.shape["ladder"])
    return jax.shard_map(body, mesh=mesh, in_specs=in_specs, out_specs=out_specs, check_vma=False)
```

```python
import functools

import jax
import jax.numpy as jnp
from jax import lax
from jax.experimental import pallas as pl
from jax.experimental.pallas import tpu as pltpu
from jax.sharding import PartitionSpec as P

F32 = jnp.float32
BF16 = jnp.bfloat16


def chunk_sizes(per_hub):
    sizes = []
    left = per_hub
    for share in (6, 20, 12, 6, 2):
        size = min(left, max(1, share * per_hub // 48))
        if size:
            sizes.append(size)
            left -= size
    if left:
        sizes.append(left)
    return sizes


def radices(count):
    steps = []
    while count > 1:
        step = 2 if not steps and count % 2 == 0 else next(r for r in (4, 2, 3, 5, count) if count % r == 0)
        steps.append(step)
        count //= step
    return steps


def turned(size, stride, radix, shift):
    perm = []
    for source in range(size):
        digit = source // stride % radix
        perm.append((source, source + ((digit + shift) % radix - digit) * stride))
    return perm


def products_kernel(cycle_scale, count, offset_ref, *refs):
    *refs, total_ref, block_ref, turned_ref, cycle_ref = refs
    parts, (lam_ref, lam_sum_ref, *start_ref) = refs[:count], refs[count:]
    group, rows, virt = parts[0].shape
    pairs = lam_ref.shape[0]

    @pl.when(pl.program_id(0) == 0)
    def _():
        total_ref[...] = start_ref[0][...] if start_ref else jnp.zeros_like(total_ref)
        cycle_ref[...] = jnp.zeros_like(cycle_ref)

    for q in range(group):
        for at, part in enumerate(parts):
            block_ref[q, at * rows : (at + 1) * rows, :] = part[q]
        turned_ref[q] = block_ref[q].T
        wide = block_ref[q].astype(F32)
        weight = jnp.sum(wide * lam_sum_ref[...], keepdims=True)
        cycle_ref[...] += weight * wide

    for pair in range(pairs):
        total = total_ref[pair]
        for q in range(group):
            half = jnp.dot(lam_ref[pair], turned_ref[q], preferred_element_type=F32).astype(BF16)
            total += jnp.dot(block_ref[q], half, preferred_element_type=F32)
        total_ref[pair] = total

    @pl.when(pl.program_id(0) == pl.num_programs(0) - 1)
    def _():
        cycle = cycle_ref[...].T.astype(BF16)
        for pair in range(pairs):
            for at in range(count):
                own = pl.ds(pl.multiple_of(offset_ref[1 + at], rows), rows)
                term = jnp.dot(lam_ref[pair, own, :], cycle, preferred_element_type=F32)
                total_ref[pair, at * rows : (at + 1) * rows, :] += cycle_scale * term


def products(size, begin, offset, factors, near, far, lam_turned, lam_sum, total):
    rows, virt = factors.shape[1:]
    pairs = lam_turned.shape[0]
    group = 2 if size % 2 == 0 and begin % 2 == 0 and near.shape[0] % 2 == 0 else 1
    first = begin // group
    whole = pl.BlockSpec((pairs, virt, virt), lambda p, o: (0, 0, 0))
    shape = (group, rows, virt)
    operands = [factors, near, *far, lam_turned, lam_sum]
    in_specs = [
        pl.BlockSpec(shape, lambda p, o: (o[0] // group + first + p, 0, 0)),
        pl.BlockSpec(shape, lambda p, o: (first + p, 0, 0)),
        *[pl.BlockSpec(shape, lambda p, o: (p, 0, 0)) for _ in far],
        whole,
        pl.BlockSpec((virt, virt), lambda p, o: (0, 0)),
    ]
    if total is not None:
        operands.append(total)
        in_specs.append(whole)
    return pl.pallas_call(
        functools.partial(products_kernel, float(pairs * virt) ** (-0.5), 2 + len(far)),
        grid_spec=pltpu.PrefetchScalarGridSpec(
            num_scalar_prefetch=1,
            grid=(size // group,),
            in_specs=in_specs,
            out_specs=whole,
            scratch_shapes=[
                pltpu.VMEM((group, virt, virt), BF16),
                pltpu.VMEM((group, virt, virt), BF16),
                pltpu.VMEM((virt, virt), F32),
            ],
        ),
        out_shape=jax.ShapeDtypeStruct((pairs, virt, virt), F32),
        input_output_aliases={} if total is None else {len(operands): 0},
        compiler_params=pltpu.CompilerParams(vmem_limit_bytes=48 << 20),
        cost_estimate=pl.CostEstimate(flops=size << 20, bytes_accessed=1 << 20, transcendentals=0),
    )(offset, *operands)


def per_device(pair_size, ladder_size, factors, lambdas):
    own_aux, rows, virt = factors.shape
    pairs = lambdas.shape[0]
    pair_index = lax.axis_index("pair")
    ladder_index = lax.axis_index("ladder")
    cols = virt // pair_size
    per_hub = own_aux // ladder_size
    sizes = chunk_sizes(per_hub)
    begins = [sum(sizes[:place]) for place in range(len(sizes))]

    def swap(array, flip):
        return lax.ppermute(array, "ladder", [(source, source ^ flip) for source in range(ladder_size)])

    def cut(index, flip, begin, size):
        return lax.dynamic_slice_in_dim(factors, (index ^ flip) * per_hub + begin, size, 0)

    flips = range(2, ladder_size)

    def exchange(place, index):
        return [swap(cut(index, flip, begins[place], sizes[place]), flip) for flip in flips]

    first = [cut(ladder_index, flip, begins[0], sizes[0]) for flip in flips]
    index, first = lax.optimization_barrier((ladder_index, first))
    far = [[swap(part, flip) for part, flip in zip(first, flips)], exchange(1, index)]
    near = swap(cut(index, 1, 0, per_hub), 1)
    lam_all = lax.all_gather(lambdas, "pair", axis=1, tiled=True)
    lam_turned = jnp.swapaxes(lam_all, 1, 2)
    places = [ladder_index * per_hub] + [(ladder_index ^ flip) * rows for flip in range(ladder_size)]
    offset = jnp.stack(places).astype(jnp.int32)
    lam_sum = jnp.sum(lam_all.astype(F32), axis=0)
    lam_sum = jnp.concatenate([lax.dynamic_slice_in_dim(lam_sum, start, rows, 0) for start in places[1:]])

    total = None
    for place, size in enumerate(sizes):
        if place + 2 < len(sizes):
            if place:
                index, total = lax.optimization_barrier((index, total))
            index, far[place] = lax.optimization_barrier((index, far[place]))
            far.append(exchange(place + 2, index))
        total = products(size, begins[place], offset, factors, near, far[place], lam_turned, lam_sum, total)

    stride = 1
    low = pair_size // ladder_size
    for radix in radices(low):
        low //= radix
        digit = pair_index // stride % radix
        view = total.reshape(pairs, ladder_size, low, radix, cols, virt)
        total = lax.dynamic_index_in_dim(view, digit, 3, keepdims=False)
        for shift in range(1, radix):
            part = lax.dynamic_index_in_dim(view, (digit + shift) % radix, 3, keepdims=False)
            part = lax.ppermute(part.astype(BF16), "pair", turned(pair_size, stride, radix, shift))
            total = total + part.astype(F32)
        stride *= radix
    digit = pair_index // stride
    view = total.reshape(pairs, ladder_size, cols, virt)
    total = None
    for flip in range(ladder_size):
        part = lax.dynamic_index_in_dim(view, ladder_index ^ digit ^ flip, 1, keepdims=False)
        if flip:
            perm = [(source, source ^ (flip * stride)) for source in range(pair_size)]
            part = lax.ppermute(part.astype(BF16), "pair", perm).astype(F32)
        total = part if total is None else total + part

    result = None
    for flip in range(ladder_size):
        part = lax.slice_in_dim(total, flip * rows, (flip + 1) * rows, axis=2)
        if flip:
            part = swap(part.astype(BF16), flip).astype(F32)
        result = part if result is None else result + part
    return jnp.swapaxes(result.astype(BF16), 0, 1)


def solution(mesh):
    in_specs = (P("pair", "ladder", None), P(None, "pair", None))
    out_specs = P("pair", None, "ladder")
    body = functools.partial(per_device, mesh.shape["pair"], mesh.shape["ladder"])
    return jax.shard_map(body, mesh=mesh, in_specs=in_specs, out_specs=out_specs, check_vma=False)
```

```python
import functools

import jax
import jax.numpy as jnp
from jax import lax
from jax.experimental import pallas as pl
from jax.experimental.pallas import tpu as pltpu
from jax.sharding import PartitionSpec as P

F32 = jnp.float32
BF16 = jnp.bfloat16


def chunk_sizes(per_hub):
    sizes = []
    left = per_hub
    for share in (14, 14, 12, 6):
        size = min(left, max(1, share * per_hub // 48))
        if size:
            sizes.append(size)
            left -= size
    if left:
        sizes.append(left)
    return sizes


def radices(count):
    steps = []
    while count > 1:
        step = 2 if not steps and count % 2 == 0 else next(r for r in (4, 2, 3, 5, count) if count % r == 0)
        steps.append(step)
        count //= step
    return steps


def turned(size, stride, radix, shift):
    perm = []
    for source in range(size):
        digit = source // stride % radix
        perm.append((source, source + ((digit + shift) % radix - digit) * stride))
    return perm


def products_kernel(cycle_scale, count, offset_ref, *refs):
    *refs, total_ref, block_ref, turned_ref, cycle_ref = refs
    parts, (lam_ref, lam_sum_ref, *start_ref) = refs[:count], refs[count:]
    group, rows, virt = parts[0].shape
    pairs = lam_ref.shape[0]

    @pl.when(pl.program_id(0) == 0)
    def _():
        total_ref[...] = start_ref[0][...] if start_ref else jnp.zeros_like(total_ref)
        cycle_ref[...] = jnp.zeros_like(cycle_ref)

    for q in range(group):
        for at, part in enumerate(parts):
            block_ref[q, at * rows : (at + 1) * rows, :] = part[q]
        turned_ref[q] = block_ref[q].T
        wide = block_ref[q].astype(F32)
        weight = jnp.sum(wide * lam_sum_ref[...], keepdims=True)
        cycle_ref[...] += weight * wide

    for pair in range(pairs):
        total = total_ref[pair]
        for q in range(group):
            half = jnp.dot(lam_ref[pair], turned_ref[q], preferred_element_type=F32).astype(BF16)
            total += jnp.dot(block_ref[q], half, preferred_element_type=F32)
        total_ref[pair] = total

    @pl.when(pl.program_id(0) == pl.num_programs(0) - 1)
    def _():
        cycle = cycle_ref[...].T.astype(BF16)
        for pair in range(pairs):
            for at in range(count):
                own = pl.ds(pl.multiple_of(offset_ref[1 + at], rows), rows)
                term = jnp.dot(lam_ref[pair, own, :], cycle, preferred_element_type=F32)
                total_ref[pair, at * rows : (at + 1) * rows, :] += cycle_scale * term


def products(size, begin, offset, factors, near, far, lam_turned, lam_sum, total):
    rows, virt = factors.shape[1:]
    pairs = lam_turned.shape[0]
    group = 1 if any(count % 2 for count in (size, begin, near.shape[0])) else 2
    first = begin // group
    whole = pl.BlockSpec((pairs, virt, virt), lambda p, o: (0, 0, 0))
    shape = (group, rows, virt)
    operands = [factors, near, *far, lam_turned, lam_sum]
    in_specs = [
        pl.BlockSpec(shape, lambda p, o: (o[0] // group + first + p, 0, 0)),
        pl.BlockSpec(shape, lambda p, o: (first + p, 0, 0)),
        *[pl.BlockSpec(shape, lambda p, o: (p, 0, 0)) for _ in far],
        whole,
        pl.BlockSpec((virt, virt), lambda p, o: (0, 0)),
    ]
    if total is not None:
        operands.append(total)
        in_specs.append(whole)
    return pl.pallas_call(
        functools.partial(products_kernel, float(pairs * virt) ** (-0.5), 2 + len(far)),
        grid_spec=pltpu.PrefetchScalarGridSpec(
            num_scalar_prefetch=1,
            grid=(size // group,),
            in_specs=in_specs,
            out_specs=whole,
            scratch_shapes=[
                pltpu.VMEM((group, virt, virt), BF16),
                pltpu.VMEM((group, virt, virt), BF16),
                pltpu.VMEM((virt, virt), F32),
            ],
        ),
        out_shape=jax.ShapeDtypeStruct((pairs, virt, virt), F32),
        input_output_aliases={} if total is None else {len(operands): 0},
        compiler_params=pltpu.CompilerParams(vmem_limit_bytes=48 << 20),
        cost_estimate=pl.CostEstimate(flops=1, bytes_accessed=1, transcendentals=0),
    )(offset, *operands)


def per_device(pair_size, ladder_size, factors, lambdas):
    own_aux, rows, virt = factors.shape
    pairs = lambdas.shape[0]
    pair_index = lax.axis_index("pair")
    ladder_index = lax.axis_index("ladder")
    cols = virt // pair_size
    per_hub = own_aux // ladder_size
    sizes = chunk_sizes(per_hub)
    begins = [sum(sizes[:place]) for place in range(len(sizes))]

    def swap(array, flip):
        return lax.ppermute(array, "ladder", [(source, source ^ flip) for source in range(ladder_size)])

    def cut(index, flip, begin, size):
        return lax.dynamic_slice_in_dim(factors, (index ^ flip) * per_hub + begin, size, 0)

    flips = range(2, ladder_size)

    def exchange(place, index):
        return [swap(cut(index, flip, begins[place], sizes[place]), flip) for flip in flips]

    first = [cut(ladder_index, flip, begins[0], sizes[0]) for flip in flips]
    index, first = lax.optimization_barrier((ladder_index, first))
    far = [[swap(part, flip) for part, flip in zip(first, flips)]]
    second = [cut(index, flip, begins[1], sizes[1]) for flip in flips]
    index, second = lax.optimization_barrier((index, second))
    far.append([swap(part, flip) for part, flip in zip(second, flips)])

    near = swap(cut(index, 1, 0, per_hub), 1)
    lam_all = lax.all_gather(lambdas, "pair", axis=1, tiled=True)
    lam_turned = jnp.swapaxes(lam_all, 1, 2)
    places = [ladder_index * per_hub] + [(ladder_index ^ flip) * rows for flip in range(ladder_size)]
    offset = jnp.stack(places).astype(jnp.int32)
    lam_sum = jnp.sum(lam_all.astype(F32), axis=0)
    lam_sum = jnp.concatenate([lax.dynamic_slice_in_dim(lam_sum, start, rows, 0) for start in places[1:]])

    total = None
    for place, size in enumerate(sizes):
        if place + 2 < len(sizes):
            if place > 1:
                index, total = lax.optimization_barrier((index, total))
            index, far[place] = lax.optimization_barrier((index, far[place]))
            far.append(exchange(place + 2, index))
        total = products(size, begins[place], offset, factors, near, far[place], lam_turned, lam_sum, total)

    stride = 1
    low = pair_size // ladder_size
    for radix in radices(low):
        low //= radix
        digit = pair_index // stride % radix
        view = total.reshape(pairs, ladder_size, low, radix, cols, virt)
        total = lax.dynamic_index_in_dim(view, digit, 3, keepdims=False)
        for shift in range(1, radix):
            part = lax.dynamic_index_in_dim(view, (digit + shift) % radix, 3, keepdims=False)
            part = lax.ppermute(part.astype(BF16), "pair", turned(pair_size, stride, radix, shift))
            total = total + part.astype(F32)
        stride *= radix
    digit = pair_index // stride
    view = total.reshape(pairs, ladder_size, cols, virt)
    total = None
    for flip in range(ladder_size):
        part = lax.dynamic_index_in_dim(view, ladder_index ^ digit ^ flip, 1, keepdims=False)
        if flip:
            perm = [(source, source ^ (flip * stride)) for source in range(pair_size)]
            part = lax.ppermute(part.astype(BF16), "pair", perm).astype(F32)
        total = part if total is None else total + part

    result = None
    for flip in range(ladder_size):
        part = lax.slice_in_dim(total, flip * rows, (flip + 1) * rows, axis=2)
        if flip:
            part = swap(part.astype(BF16), flip).astype(F32)
        result = part if result is None else result + part
    return jnp.swapaxes(result.astype(BF16), 0, 1)


def solution(mesh):
    in_specs = (P("pair", "ladder", None), P(None, "pair", None))
    out_specs = P("pair", None, "ladder")
    body = functools.partial(per_device, mesh.shape["pair"], mesh.shape["ladder"])
    return jax.shard_map(body, mesh=mesh, in_specs=in_specs, out_specs=out_specs, check_vma=False)
```

```python
import functools

import jax
import jax.numpy as jnp
from jax import lax
from jax.experimental import pallas as pl
from jax.experimental.pallas import tpu as pltpu
from jax.sharding import PartitionSpec as P

F32 = jnp.float32
BF16 = jnp.bfloat16


def chunk_sizes(per_hub):
    sizes = []
    left = per_hub
    for share in (14, 12, 10, 6, 4):
        size = min(left, max(1, share * per_hub // 48))
        if size:
            sizes.append(size)
            left -= size
    if left:
        sizes.append(left)
    return sizes


def radices(count):
    steps = []
    while count > 1:
        step = 2 if not steps and count % 2 == 0 else next(r for r in (4, 2, 3, 5, count) if count % r == 0)
        steps.append(step)
        count //= step
    return steps


def turned(size, stride, radix, shift):
    perm = []
    for source in range(size):
        digit = source // stride % radix
        perm.append((source, source + ((digit + shift) % radix - digit) * stride))
    return perm


def products_kernel(cycle_scale, count, has_start, split, offset_ref, *refs):
    if split:
        *refs, keep_ref, send_ref, block_ref, turned_ref, cycle_ref, total_ref = refs
    else:
        *refs, total_ref, block_ref, turned_ref, cycle_ref = refs
    parts, lam_ref, lam_sum_ref = refs[:count], refs[count], refs[count + 1]
    group, rows, virt = parts[0].shape
    pairs = lam_ref.shape[0]

    @pl.when(pl.program_id(0) == 0)
    def _():
        total_ref[...] = refs[count + 2][...] if has_start else jnp.zeros_like(total_ref)
        cycle_ref[...] = jnp.zeros_like(cycle_ref)

    for q in range(group):
        for at, part in enumerate(parts):
            block_ref[q, at * rows : (at + 1) * rows, :] = part[q]
        turned_ref[q] = block_ref[q].T
        wide = block_ref[q].astype(F32)
        weight = jnp.sum(wide * lam_sum_ref[...], keepdims=True)
        cycle_ref[...] += weight * wide

    for pair in range(pairs):
        total = total_ref[pair]
        for q in range(group):
            half = jnp.dot(lam_ref[pair], turned_ref[q], preferred_element_type=F32).astype(BF16)
            total += jnp.dot(block_ref[q], half, preferred_element_type=F32)
        total_ref[pair] = total

    @pl.when(pl.program_id(0) == pl.num_programs(0) - 1)
    def _():
        cycle = cycle_ref[...].T.astype(BF16)
        for pair in range(pairs):
            for at in range(count):
                own = pl.ds(pl.multiple_of(offset_ref[1 + at], rows), rows)
                term = jnp.dot(lam_ref[pair, own, :], cycle, preferred_element_type=F32)
                total_ref[pair, at * rows : (at + 1) * rows, :] += cycle_scale * term
        if split:
            _, _, high, cols, _ = keep_ref.shape
            digit = offset_ref[1 + count]
            for pair in range(pairs):
                for at in range(count):
                    for place in range(high):
                        start = at * rows + 2 * place * cols
                        own = pl.ds(pl.multiple_of(start + digit * cols, cols), cols)
                        other = pl.ds(pl.multiple_of(start + (1 - digit) * cols, cols), cols)
                        keep_ref[pair, at, place] = total_ref[pair, own, :]
                        send_ref[pair, at, place] = total_ref[pair, other, :].astype(BF16)


def products(size, begin, offset, factors, near, far, lam_turned, lam_sum, total, halves=None):
    rows, virt = factors.shape[1:]
    pairs = lam_turned.shape[0]
    group = 1 if any(count % 2 for count in (size, begin, near.shape[0])) else 2
    first = begin // group
    whole = pl.BlockSpec((pairs, virt, virt), lambda p, o: (0, 0, 0))
    shape = (group, rows, virt)
    operands = [factors, near, *far, lam_turned, lam_sum]
    in_specs = [
        pl.BlockSpec(shape, lambda p, o: (o[0] // group + first + p, 0, 0)),
        pl.BlockSpec(shape, lambda p, o: (first + p, 0, 0)),
        *[pl.BlockSpec(shape, lambda p, o: (p, 0, 0)) for _ in far],
        whole,
        pl.BlockSpec((virt, virt), lambda p, o: (0, 0)),
    ]
    if total is not None:
        operands.append(total)
        in_specs.append(whole)
    scratch_shapes = [
        pltpu.VMEM((group, virt, virt), BF16),
        pltpu.VMEM((group, virt, virt), BF16),
        pltpu.VMEM((virt, virt), F32),
    ]
    if halves is None:
        out_specs, out_shape = whole, jax.ShapeDtypeStruct((pairs, virt, virt), F32)
    else:
        out_specs = [pl.BlockSpec(halves, lambda p, o: (0, 0, 0, 0, 0))] * 2
        out_shape = [jax.ShapeDtypeStruct(halves, F32), jax.ShapeDtypeStruct(halves, BF16)]
        scratch_shapes.append(pltpu.VMEM((pairs, virt, virt), F32))
    return pl.pallas_call(
        functools.partial(
            products_kernel, float(pairs * virt) ** (-0.5), 2 + len(far), total is not None, halves is not None
        ),
        grid_spec=pltpu.PrefetchScalarGridSpec(
            num_scalar_prefetch=1,
            grid=(size // group,),
            in_specs=in_specs,
            out_specs=out_specs,
            scratch_shapes=scratch_shapes,
        ),
        out_shape=out_shape,
        input_output_aliases={len(operands): 0} if total is not None and halves is None else {},
        compiler_params=pltpu.CompilerParams(vmem_limit_bytes=48 << 20),
        cost_estimate=pl.CostEstimate(flops=1, bytes_accessed=1, transcendentals=0),
    )(offset, *operands)


def per_device(pair_size, ladder_size, factors, lambdas):
    own_aux, rows, virt = factors.shape
    pairs = lambdas.shape[0]
    pair_index = lax.axis_index("pair")
    ladder_index = lax.axis_index("ladder")
    cols = virt // pair_size
    per_hub = own_aux // ladder_size
    sizes = chunk_sizes(per_hub)
    begins = [sum(sizes[:place]) for place in range(len(sizes))]

    def swap(array, flip):
        return lax.ppermute(array, "ladder", [(source, source ^ flip) for source in range(ladder_size)])

    def cut(index, flip, begin, size):
        return lax.dynamic_slice_in_dim(factors, (index ^ flip) * per_hub + begin, size, 0)

    flips = range(2, ladder_size)

    def exchange(place, index):
        return [swap(cut(index, flip, begins[place], sizes[place]), flip) for flip in flips]

    first = [cut(ladder_index, flip, begins[0], sizes[0]) for flip in flips]
    index, first = lax.optimization_barrier((ladder_index, first))
    far = [[swap(part, flip) for part, flip in zip(first, flips)]]
    second = [cut(index, flip, begins[1], sizes[1]) for flip in flips]
    index, second = lax.optimization_barrier((index, second))
    far.append([swap(part, flip) for part, flip in zip(second, flips)])

    near = swap(cut(index, 1, 0, per_hub), 1)
    lam_all = lax.all_gather(lambdas, "pair", axis=1, tiled=True)
    lam_turned = jnp.swapaxes(lam_all, 1, 2)
    places = [ladder_index * per_hub] + [(ladder_index ^ flip) * rows for flip in range(ladder_size)]
    offset = jnp.stack(places + [pair_index % 2]).astype(jnp.int32)
    lam_sum = jnp.sum(lam_all.astype(F32), axis=0)
    lam_sum = jnp.concatenate([lax.dynamic_slice_in_dim(lam_sum, start, rows, 0) for start in places[1:]])

    def digit_sum(total, stride, low, radix):
        digit = pair_index // stride % radix
        view = total.reshape(pairs, ladder_size, low // radix, radix, cols, virt)
        total = lax.dynamic_index_in_dim(view, digit, 3, keepdims=False)
        for shift in range(1, radix):
            part = lax.dynamic_index_in_dim(view, (digit + shift) % radix, 3, keepdims=False)
            part = lax.ppermute(part.astype(BF16), "pair", turned(pair_size, stride, radix, shift))
            total = total + part.astype(F32)
        return total

    low = pair_size // ladder_size
    steps = radices(low)
    halves = None
    if steps[:1] == [2] and cols % 16 == 0:
        halves = (pairs, ladder_size, low // 2, cols, virt)

    total = None
    for place, size in enumerate(sizes):
        if place + 2 < len(sizes):
            if place:
                index, total = lax.optimization_barrier((index, total))
            index, far[place] = lax.optimization_barrier((index, far[place]))
            far.append(exchange(place + 2, index))
        total = products(
            size, begins[place], offset, factors, near, far[place], lam_turned, lam_sum, total,
            halves if place + 1 == len(sizes) else None,
        )

    stride = 1
    if halves:
        keep, send = total
        total = keep + lax.ppermute(send, "pair", turned(pair_size, 1, 2, 1)).astype(F32)
        stride, low, steps = 2, low // 2, steps[1:]
    for radix in steps:
        total = digit_sum(total, stride, low, radix)
        stride, low = stride * radix, low // radix
    digit = pair_index // stride
    view = total.reshape(pairs, ladder_size, cols, virt)
    total = None
    for flip in range(ladder_size):
        part = lax.dynamic_index_in_dim(view, ladder_index ^ digit ^ flip, 1, keepdims=False)
        if flip:
            perm = [(source, source ^ (flip * stride)) for source in range(pair_size)]
            part = lax.ppermute(part.astype(BF16), "pair", perm).astype(F32)
        total = part if total is None else total + part

    result = None
    for flip in range(ladder_size):
        part = lax.slice_in_dim(total, flip * rows, (flip + 1) * rows, axis=2)
        if flip:
            part = swap(part.astype(BF16), flip).astype(F32)
        result = part if result is None else result + part
    return jnp.swapaxes(result.astype(BF16), 0, 1)


def solution(mesh):
    in_specs = (P("pair", "ladder", None), P(None, "pair", None))
    out_specs = P("pair", None, "ladder")
    body = functools.partial(per_device, mesh.shape["pair"], mesh.shape["ladder"])
    return jax.shard_map(body, mesh=mesh, in_specs=in_specs, out_specs=out_specs, check_vma=False)
```

```python
import functools

import jax
import jax.numpy as jnp
from jax import lax
from jax.experimental import pallas as pl
from jax.experimental.pallas import tpu as pltpu
from jax.sharding import PartitionSpec as P

F32 = jnp.float32
BF16 = jnp.bfloat16


def chunk_sizes(per_hub):
    sizes = []
    left = per_hub
    for share in (4, 14, 12, 10, 6):
        size = min(left, max(1, share * per_hub // 48))
        if size:
            sizes.append(size)
            left -= size
    if left:
        sizes.append(left)
    return sizes


def radices(count):
    steps = []
    while count > 1:
        step = 2 if not steps and count % 2 == 0 else next(r for r in (4, 2, 3, 5, count) if count % r == 0)
        steps.append(step)
        count //= step
    return steps


def turned(size, stride, radix, shift):
    perm = []
    for source in range(size):
        digit = source // stride % radix
        perm.append((source, source + ((digit + shift) % radix - digit) * stride))
    return perm


def products_kernel(cycle_scale, count, has_start, split, offset_ref, *refs):
    if split:
        *refs, keep_ref, send_ref, block_ref, turned_ref, cycle_ref, total_ref = refs
    else:
        *refs, total_ref, block_ref, turned_ref, cycle_ref = refs
    parts, lam_ref, lam_sum_ref = refs[:count], refs[count], refs[count + 1]
    group, rows, virt = parts[0].shape
    pairs = lam_ref.shape[0]

    @pl.when(pl.program_id(0) == 0)
    def _():
        total_ref[...] = refs[count + 2][...] if has_start else jnp.zeros_like(total_ref)
        cycle_ref[...] = jnp.zeros_like(cycle_ref)

    for q in range(group):
        for at, part in enumerate(parts):
            block_ref[q, at * rows : (at + 1) * rows, :] = part[q]
        turned_ref[q] = block_ref[q].T
        wide = block_ref[q].astype(F32)
        weight = jnp.sum(wide * lam_sum_ref[...], keepdims=True)
        cycle_ref[...] += weight * wide

    for pair in range(pairs):
        total = total_ref[pair]
        for q in range(group):
            half = jnp.dot(lam_ref[pair], turned_ref[q], preferred_element_type=F32).astype(BF16)
            total += jnp.dot(block_ref[q], half, preferred_element_type=F32)
        total_ref[pair] = total

    @pl.when(pl.program_id(0) == pl.num_programs(0) - 1)
    def _():
        cycle = cycle_ref[...].T.astype(BF16)
        for pair in range(pairs):
            for at in range(count):
                own = pl.ds(pl.multiple_of(offset_ref[1 + at], rows), rows)
                term = jnp.dot(lam_ref[pair, own, :], cycle, preferred_element_type=F32)
                total_ref[pair, at * rows : (at + 1) * rows, :] += cycle_scale * term
        if split:
            _, _, high, cols, _ = keep_ref.shape
            digit = offset_ref[1 + count]
            for pair in range(pairs):
                for at in range(count):
                    for place in range(high):
                        start = at * rows + 2 * place * cols
                        own = pl.ds(pl.multiple_of(start + digit * cols, cols), cols)
                        other = pl.ds(pl.multiple_of(start + (1 - digit) * cols, cols), cols)
                        keep_ref[pair, at, place] = total_ref[pair, own, :]
                        send_ref[pair, at, place] = total_ref[pair, other, :].astype(BF16)


def products(size, begin, offset, factors, near, far, lam_turned, lam_sum, total, halves=None):
    rows, virt = factors.shape[1:]
    pairs = lam_turned.shape[0]
    group = 1 if any(count % 2 for count in (size, begin, near.shape[0])) else 2
    first = begin // group
    whole = pl.BlockSpec((pairs, virt, virt), lambda p, o: (0, 0, 0))
    shape = (group, rows, virt)
    operands = [factors, near, *far, lam_turned, lam_sum]
    in_specs = [
        pl.BlockSpec(shape, lambda p, o: (o[0] // group + first + p, 0, 0)),
        pl.BlockSpec(shape, lambda p, o: (first + p, 0, 0)),
        *[pl.BlockSpec(shape, lambda p, o: (p, 0, 0)) for _ in far],
        whole,
        pl.BlockSpec((virt, virt), lambda p, o: (0, 0)),
    ]
    if total is not None:
        operands.append(total)
        in_specs.append(whole)
    scratch_shapes = [
        pltpu.VMEM((group, virt, virt), BF16),
        pltpu.VMEM((group, virt, virt), BF16),
        pltpu.VMEM((virt, virt), F32),
    ]
    if halves is None:
        out_specs, out_shape = whole, jax.ShapeDtypeStruct((pairs, virt, virt), F32)
    else:
        out_specs = [pl.BlockSpec(halves, lambda p, o: (0, 0, 0, 0, 0))] * 2
        out_shape = [jax.ShapeDtypeStruct(halves, F32), jax.ShapeDtypeStruct(halves, BF16)]
        scratch_shapes.append(pltpu.VMEM((pairs, virt, virt), F32))
    return pl.pallas_call(
        functools.partial(
            products_kernel, float(pairs * virt) ** (-0.5), 2 + len(far), total is not None, halves is not None
        ),
        grid_spec=pltpu.PrefetchScalarGridSpec(
            num_scalar_prefetch=1,
            grid=(size // group,),
            in_specs=in_specs,
            out_specs=out_specs,
            scratch_shapes=scratch_shapes,
        ),
        out_shape=out_shape,
        input_output_aliases={len(operands): 0} if total is not None and halves is None else {},
        compiler_params=pltpu.CompilerParams(vmem_limit_bytes=48 << 20),
        cost_estimate=pl.CostEstimate(flops=1, bytes_accessed=1, transcendentals=0),
    )(offset, *operands)


def per_device(pair_size, ladder_size, factors, lambdas):
    own_aux, rows, virt = factors.shape
    pairs = lambdas.shape[0]
    pair_index = lax.axis_index("pair")
    ladder_index = lax.axis_index("ladder")
    cols = virt // pair_size
    per_hub = own_aux // ladder_size
    sizes = chunk_sizes(per_hub)
    begins = [sum(sizes[:place]) for place in range(len(sizes))]

    def swap(array, flip):
        return lax.ppermute(array, "ladder", [(source, source ^ flip) for source in range(ladder_size)])

    def cut(index, flip, begin, size):
        return lax.dynamic_slice_in_dim(factors, (index ^ flip) * per_hub + begin, size, 0)

    flips = range(2, ladder_size)

    def exchange(place, index):
        return [swap(cut(index, flip, begins[place], sizes[place]), flip) for flip in flips]

    first = [cut(ladder_index, flip, begins[0], sizes[0]) for flip in flips]
    far = [[swap(part, flip) for part, flip in zip(first, flips)]]
    lam_all = lax.all_gather(lambdas, "pair", axis=1, tiled=True)
    index, first = lax.optimization_barrier((ladder_index, first))
    second = [cut(index, 1, 0, per_hub)] + [cut(index, flip, begins[1], sizes[1]) for flip in flips]
    lam_all, second = lax.optimization_barrier((lam_all, second))
    lam_turned = jnp.swapaxes(lam_all, 1, 2)
    lam_sum = jnp.sum(lam_all.astype(F32), axis=0)
    second, far[0] = lax.optimization_barrier((second, far[0]))
    near, *others = [swap(part, flip) for flip, part in enumerate(second, 1)]
    far.append(others)

    places = [ladder_index * per_hub] + [(ladder_index ^ flip) * rows for flip in range(ladder_size)]
    offset = jnp.stack(places + [pair_index % 2]).astype(jnp.int32)
    lam_sum = jnp.concatenate([lax.dynamic_slice_in_dim(lam_sum, start, rows, 0) for start in places[1:]])

    def digit_sum(total, stride, low, radix):
        digit = pair_index // stride % radix
        view = total.reshape(pairs, ladder_size, low // radix, radix, cols, virt)
        total = lax.dynamic_index_in_dim(view, digit, 3, keepdims=False)
        for shift in range(1, radix):
            part = lax.dynamic_index_in_dim(view, (digit + shift) % radix, 3, keepdims=False)
            part = lax.ppermute(part.astype(BF16), "pair", turned(pair_size, stride, radix, shift))
            total = total + part.astype(F32)
        return total

    low = pair_size // ladder_size
    steps = radices(low)
    halves = None
    if steps[:1] == [2] and cols % 16 == 0:
        halves = (pairs, ladder_size, low // 2, cols, virt)

    total = None
    for place, size in enumerate(sizes):
        if place + 2 < len(sizes):
            if place:
                index, total = lax.optimization_barrier((index, total))
            index, far[place] = lax.optimization_barrier((index, far[place]))
            far.append(exchange(place + 2, index))
        total = products(
            size, begins[place], offset, factors, near, far[place], lam_turned, lam_sum, total,
            halves if place + 1 == len(sizes) else None,
        )

    stride = 1
    if halves:
        keep, send = total
        total = keep + lax.ppermute(send, "pair", turned(pair_size, 1, 2, 1)).astype(F32)
        stride, low, steps = 2, low // 2, steps[1:]
    for radix in steps:
        total = digit_sum(total, stride, low, radix)
        stride, low = stride * radix, low // radix
    digit = pair_index // stride
    view = total.reshape(pairs, ladder_size, cols, virt)
    total = None
    for flip in range(ladder_size):
        part = lax.dynamic_index_in_dim(view, ladder_index ^ digit ^ flip, 1, keepdims=False)
        if flip:
            perm = [(source, source ^ (flip * stride)) for source in range(pair_size)]
            part = lax.ppermute(part.astype(BF16), "pair", perm).astype(F32)
        total = part if total is None else total + part

    result = None
    for flip in range(ladder_size):
        part = lax.slice_in_dim(total, flip * rows, (flip + 1) * rows, axis=2)
        if flip:
            part = swap(part.astype(BF16), flip).astype(F32)
        result = part if result is None else result + part
    return jnp.swapaxes(result.astype(BF16), 0, 1)


def solution(mesh):
    in_specs = (P("pair", "ladder", None), P(None, "pair", None))
    out_specs = P("pair", None, "ladder")
    body = functools.partial(per_device, mesh.shape["pair"], mesh.shape["ladder"])
    return jax.shard_map(body, mesh=mesh, in_specs=in_specs, out_specs=out_specs, check_vma=False)
```

```python
import functools

import jax
import jax.numpy as jnp
from jax import lax
from jax.experimental import pallas as pl
from jax.experimental.pallas import tpu as pltpu
from jax.sharding import PartitionSpec as P

F32 = jnp.float32
BF16 = jnp.bfloat16


def chunk_sizes(per_hub):
    sizes = []
    left = per_hub
    for share in (4, 16, 14, 8, 4):
        size = min(left, max(1, share * per_hub // 48))
        if size:
            sizes.append(size)
            left -= size
    if left:
        sizes.append(left)
    return sizes


def radices(count):
    steps = []
    while count > 1:
        step = 2 if not steps and count % 2 == 0 else next(r for r in (4, 2, 3, 5, count) if count % r == 0)
        steps.append(step)
        count //= step
    return steps


def turned(size, stride, radix, shift):
    perm = []
    for source in range(size):
        digit = source // stride % radix
        perm.append((source, source + ((digit + shift) % radix - digit) * stride))
    return perm


def products_kernel(cycle_scale, count, has_start, split, offset_ref, *refs):
    if split:
        *refs, keep_ref, send_ref, block_ref, turned_ref, cycle_ref, total_ref = refs
    else:
        *refs, total_ref, block_ref, turned_ref, cycle_ref = refs
    parts, lam_ref, lam_sum_ref = refs[:count], refs[count], refs[count + 1]
    group, rows, virt = parts[0].shape
    pairs = lam_ref.shape[0]

    @pl.when(pl.program_id(0) == 0)
    def _():
        total_ref[...] = refs[count + 2][...] if has_start else jnp.zeros_like(total_ref)
        cycle_ref[...] = jnp.zeros_like(cycle_ref)

    for q in range(group):
        for at, part in enumerate(parts):
            block_ref[q, at * rows : (at + 1) * rows, :] = part[q]
        turned_ref[q] = block_ref[q].T
        wide = block_ref[q].astype(F32)
        weight = jnp.sum(wide * lam_sum_ref[...], keepdims=True)
        cycle_ref[...] += weight * turned_ref[q].astype(F32)

    for pair in range(pairs):
        total = total_ref[pair]
        for q in range(group):
            half = jnp.dot(lam_ref[pair], turned_ref[q], preferred_element_type=F32).astype(BF16)
            total += jnp.dot(block_ref[q], half, preferred_element_type=F32)
        total_ref[pair] = total

    @pl.when(pl.program_id(0) == pl.num_programs(0) - 1)
    def _():
        cycle = cycle_ref[...].astype(BF16)
        for pair in range(pairs):
            for at in range(count):
                own = pl.ds(pl.multiple_of(offset_ref[1 + at], rows), rows)
                term = jnp.dot(lam_ref[pair, own, :], cycle, preferred_element_type=F32)
                total_ref[pair, at * rows : (at + 1) * rows, :] += cycle_scale * term
        if split:
            _, _, high, cols, _ = keep_ref.shape
            digit = offset_ref[1 + count]
            for pair in range(pairs):
                for at in range(count):
                    for place in range(high):
                        start = at * rows + 2 * place * cols
                        own = pl.ds(pl.multiple_of(start + digit * cols, cols), cols)
                        other = pl.ds(pl.multiple_of(start + (1 - digit) * cols, cols), cols)
                        keep_ref[pair, at, place] = total_ref[pair, own, :]
                        send_ref[pair, at, place] = total_ref[pair, other, :].astype(BF16)


def products(size, begin, offset, factors, near, far, lam_turned, lam_sum, total, halves=None):
    rows, virt = factors.shape[1:]
    pairs = lam_turned.shape[0]
    group = 1 if any(count % 2 for count in (size, begin, near.shape[0])) else 2
    first = begin // group
    whole = pl.BlockSpec((pairs, virt, virt), lambda p, o: (0, 0, 0))
    shape = (group, rows, virt)
    operands = [factors, near, *far, lam_turned, lam_sum]
    in_specs = [
        pl.BlockSpec(shape, lambda p, o: (o[0] // group + first + p, 0, 0)),
        pl.BlockSpec(shape, lambda p, o: (first + p, 0, 0)),
        *[pl.BlockSpec(shape, lambda p, o: (p, 0, 0)) for _ in far],
        whole,
        pl.BlockSpec((virt, virt), lambda p, o: (0, 0)),
    ]
    if total is not None:
        operands.append(total)
        in_specs.append(whole)
    scratch_shapes = [
        pltpu.VMEM((group, virt, virt), BF16),
        pltpu.VMEM((group, virt, virt), BF16),
        pltpu.VMEM((virt, virt), F32),
    ]
    if halves is None:
        out_specs, out_shape = whole, jax.ShapeDtypeStruct((pairs, virt, virt), F32)
    else:
        out_specs = [pl.BlockSpec(halves, lambda p, o: (0, 0, 0, 0, 0))] * 2
        out_shape = [jax.ShapeDtypeStruct(halves, F32), jax.ShapeDtypeStruct(halves, BF16)]
        scratch_shapes.append(pltpu.VMEM((pairs, virt, virt), F32))
    return pl.pallas_call(
        functools.partial(
            products_kernel, float(pairs * virt) ** (-0.5), 2 + len(far), total is not None, halves is not None
        ),
        grid_spec=pltpu.PrefetchScalarGridSpec(
            num_scalar_prefetch=1,
            grid=(size // group,),
            in_specs=in_specs,
            out_specs=out_specs,
            scratch_shapes=scratch_shapes,
        ),
        out_shape=out_shape,
        input_output_aliases={len(operands): 0} if total is not None and halves is None else {},
        compiler_params=pltpu.CompilerParams(vmem_limit_bytes=48 << 20),
        cost_estimate=pl.CostEstimate(flops=1, bytes_accessed=1, transcendentals=0),
    )(offset, *operands)


def per_device(pair_size, ladder_size, factors, lambdas):
    own_aux, rows, virt = factors.shape
    pairs = lambdas.shape[0]
    pair_index = lax.axis_index("pair")
    ladder_index = lax.axis_index("ladder")
    cols = virt // pair_size
    per_hub = own_aux // ladder_size
    sizes = chunk_sizes(per_hub)
    begins = [sum(sizes[:place]) for place in range(len(sizes))]

    def swap(array, flip):
        return lax.ppermute(array, "ladder", [(source, source ^ flip) for source in range(ladder_size)])

    def cut(index, flip, begin, size):
        return lax.dynamic_slice_in_dim(factors, (index ^ flip) * per_hub + begin, size, 0)

    flips = range(2, ladder_size)

    def exchange(place, index):
        return [swap(cut(index, flip, begins[place], sizes[place]), flip) for flip in flips]

    first = [cut(ladder_index, flip, begins[0], sizes[0]) for flip in flips]
    far = [[swap(part, flip) for part, flip in zip(first, flips)]]
    lam_all = lax.all_gather(lambdas, "pair", axis=1, tiled=True)
    index, first = lax.optimization_barrier((ladder_index, first))
    second = [cut(index, 1, 0, per_hub)] + [cut(index, flip, begins[1], sizes[1]) for flip in flips]
    lam_all, second = lax.optimization_barrier((lam_all, second))
    lam_turned = jnp.swapaxes(lam_all, 1, 2)
    lam_sum = jnp.sum(lam_all.astype(F32), axis=0)
    second, far[0] = lax.optimization_barrier((second, far[0]))
    near, *others = [swap(part, flip) for flip, part in enumerate(second, 1)]
    far.append(others)

    places = [ladder_index * per_hub] + [(ladder_index ^ flip) * rows for flip in range(ladder_size)]
    offset = jnp.stack(places + [pair_index % 2]).astype(jnp.int32)
    lam_sum = jnp.concatenate([lax.dynamic_slice_in_dim(lam_sum, start, rows, 0) for start in places[1:]])

    def digit_sum(total, stride, low, radix):
        digit = pair_index // stride % radix
        view = total.reshape(pairs, ladder_size, low // radix, radix, cols, virt)
        total = lax.dynamic_index_in_dim(view, digit, 3, keepdims=False)
        for shift in range(1, radix):
            part = lax.dynamic_index_in_dim(view, (digit + shift) % radix, 3, keepdims=False)
            part = lax.ppermute(part.astype(BF16), "pair", turned(pair_size, stride, radix, shift))
            total = total + part.astype(F32)
        return total

    low = pair_size // ladder_size
    steps = radices(low)
    halves = None
    if steps[:1] == [2] and cols % 16 == 0:
        halves = (pairs, ladder_size, low // 2, cols, virt)

    total = None
    for place, size in enumerate(sizes):
        if place + 2 < len(sizes):
            if place:
                index, total = lax.optimization_barrier((index, total))
            index, far[place] = lax.optimization_barrier((index, far[place]))
            far.append(exchange(place + 2, index))
        total = products(
            size, begins[place], offset, factors, near, far[place], lam_turned, lam_sum, total,
            halves if place + 1 == len(sizes) else None,
        )

    stride = 1
    if halves:
        keep, send = total
        total = keep + lax.ppermute(send, "pair", turned(pair_size, 1, 2, 1)).astype(F32)
        stride, low, steps = 2, low // 2, steps[1:]
    for radix in steps:
        total = digit_sum(total, stride, low, radix)
        stride, low = stride * radix, low // radix
    digit = pair_index // stride
    view = total.reshape(pairs, ladder_size, cols, virt)
    total = None
    for flip in range(ladder_size):
        part = lax.dynamic_index_in_dim(view, ladder_index ^ digit ^ flip, 1, keepdims=False)
        if flip:
            perm = [(source, source ^ (flip * stride)) for source in range(pair_size)]
            part = lax.ppermute(part.astype(BF16), "pair", perm).astype(F32)
        total = part if total is None else total + part

    result = None
    for flip in range(ladder_size):
        part = lax.slice_in_dim(total, flip * rows, (flip + 1) * rows, axis=2)
        if flip:
            part = swap(part.astype(BF16), flip).astype(F32)
        result = part if result is None else result + part
    return jnp.swapaxes(result.astype(BF16), 0, 1)


def solution(mesh):
    in_specs = (P("pair", "ladder", None), P(None, "pair", None))
    out_specs = P("pair", None, "ladder")
    body = functools.partial(per_device, mesh.shape["pair"], mesh.shape["ladder"])
    return jax.shard_map(body, mesh=mesh, in_specs=in_specs, out_specs=out_specs, check_vma=False)
```
